32 devices in a mesh: groups: 2 (over y), box: 4 (over z), angle: 2 (over x), sub: 2 (over core).
Axes of the slice: x: 2, y: 2, z: 4, core: 2. Of those that a mesh axis runs over, the one named last changes fastest.
Arguments:
- currents: bfloat16 [2, 16, 48, 256], P(None, 'angle', ('groups', 'box')), parts along dimension 2, may hold values from -6 to 6
- near_blocks: bfloat16 [2, 192, 256, 256], P(None, ('groups', 'box', 'sub')), parts along dimension 1, may hold values from -0.375 to 0.375
- near_pairs: int32 [192, 2], P(('groups', 'box', 'sub')), parts along dimension 0, may hold values from 0 to 23, as said below
- near_count: int32 [16], P(('groups', 'box', 'sub')), parts along dimension 0, may hold values from 3 to 12, as said below
- radiation: bfloat16 [2, 48, 2, 128, 256], P(None, ('groups', 'box'), 'sub'), parts along dimension 1, may hold values from -0.375 to 0.375
- parent_of: int32 [48], P('groups'), parts along dimension 0, may hold values from 0 to 7
- octant: int32 [48], P('groups'), parts along dimension 0, may hold values from 0 to 7
- far0_src: int32 [48, 16], P(('groups', 'box')), parts along dimension 0, may hold values from 0 to 23
- far0_disp: int32 [48, 16], P(('groups', 'box')), parts along dimension 0, may hold values from 0 to 315
- far1_src: int32 [16, 8], P(('groups', 'box')), parts along dimension 0, may hold values from 0 to 7
- far1_disp: int32 [16, 8], P(('groups', 'box')), parts along dimension 0, may hold values from 0 to 315
- trans0: bfloat16 [316, 2, 128], replicated, may hold values from -1.5 to 1.5
- trans1: bfloat16 [316, 2, 256], replicated, may hold values from -2 to 2
- phases: float32 [8, 256], replicated, may hold values from -3.140625 to 3.140625
- interp: float32 [256, 128], replicated, may hold values from -0.5 to 0.5
Outputs:
- field: bfloat16 [2, 16, 48, 256], P(None, 'angle', ('groups', 'box'), 'sub'), parts along dimension 2
The draws below stay inside these ranges and needn't reach their ends.
There are 2 independent parts, one for each index of `groups`. The reference program is written for one: setup_inputs(seed, part) draws one part's arguments, and reference() takes and returns one part's arrays. A program takes and returns all parts, laid end to end along the dimension named above; an argument that names none is the same for every part. Nothing has to cross between parts.
Inputs may be any that keep to these rules, and one draw needn't show every extreme that they name: `near_pairs`: slots come in blocks of 12, one block for each device of box and sub in that order; a slot's target is one of the 6 boxes of its device along box, and its source lies from the target to the target plus 6. Among live slots every unordered pair of boxes appears at most once. The first near_count[h] slots of holder h are live, the others are not used.
All inputs are finite; a program needn't handle non-finite values.
Results may differ from the reference program's by a relative error of at most 0.009.
Values may be sent and summed in bfloat16 or wider, within the bound.
A program may use at most 64 MiB of HBM per device.

```python
import jax
import jax.numpy as jnp
from jax import lax

UNK = 256
DIR0 = 128
DIR1 = 256
DISP = 316
FAR0 = 16
FAR1 = 8
SLOTS = 6
PAIR_DEV = 12
ANGLES = 16
BOXES = 24
PARENTS = 8
PAIRS = 96
N_SUB = 2


def near_layout(key):
    device_count = BOXES // SLOTS
    combos = SLOTS * (SLOTS + 1)
    code_list = jnp.arange(combos, dtype=jnp.int32)
    row_part = code_list // (SLOTS + 1)
    offset_part = code_list % (SLOTS + 1)

    def one_device(device):
        device_key = jax.random.fold_in(key, device)
        ranking = jax.random.permutation(device_key, combos).astype(jnp.int32)
        targets = device * SLOTS + row_part
        sources = targets + offset_part
        invalid = (sources >= BOXES).astype(jnp.int32)
        ordering = jnp.argsort(invalid * combos + ranking, stable=True)
        chosen = ordering[:N_SUB * PAIR_DEV]
        picked = jnp.stack([targets[chosen], jnp.minimum(sources[chosen], BOXES - 1)], axis=1)
        return (picked, combos - jnp.sum(invalid))
    pair_list, valid_count = jax.vmap(one_device)(jnp.arange(device_count, dtype=jnp.int32))
    pair_list = pair_list.reshape(device_count * N_SUB * PAIR_DEV, 2)
    holder_valid = valid_count[:, None] - jnp.arange(N_SUB, dtype=jnp.int32)[None, :] * PAIR_DEV
    holder_valid = jnp.clip(holder_valid, 0, PAIR_DEV).reshape(-1)
    drawn_count = jax.random.randint(jax.random.fold_in(key, 7), (device_count * N_SUB,), PAIR_DEV // 4, PAIR_DEV + 1)
    counts = jnp.minimum(drawn_count, holder_valid).at[0].set(PAIR_DEV)
    return (pair_list.astype(jnp.int32), counts.astype(jnp.int32))


def draw_near_pairs(key, part):
    pair_list, counts = near_layout(key)
    return pair_list


def draw_near_count(key, part):
    pair_list, counts = near_layout(key)
    return counts


def touch_ends(drawn, key, least, top_value):
    shape = drawn.shape
    place = [jax.random.randint(jax.random.fold_in(key, axis), (), 0, shape[axis]) for axis in range(len(shape))]
    drawn = drawn.at[tuple(place)].set(least)
    longest = shape.index(max(shape))
    place[longest] = (place[longest] + 1) % shape[longest]
    return drawn.at[tuple(place)].set(top_value)


def block_levels(key, shape, cuts, low, high):
    gain = 1.0
    for axis_at, parts in cuts:
        draws = jax.random.uniform(jax.random.fold_in(jax.random.fold_in(key, 6), axis_at), (parts,), jnp.float32, low / len(cuts), high / len(cuts))
        gain = gain * jnp.repeat(jnp.exp(draws), shape[axis_at] // parts).reshape((-1,) + (1,) * (len(shape) - 1 - axis_at))
    return gain


def scatter_about(stream_key, shape, deviation, bound, pieces=(), kind=jnp.bfloat16):
    factor_of = block_levels(stream_key, shape, pieces, -0.22, 0.18) if pieces else 1.0
    array = jax.random.normal(stream_key, shape, jnp.float32) * deviation * factor_of
    return jnp.minimum(jnp.maximum(array, -bound), bound).astype(kind)


def setup_inputs(seed: int = 0, part: int = 0) -> dict:
    keys = jax.random.split(jax.random.key(seed), 16)
    own_keys = jax.random.split(jax.random.fold_in(keys[15], part), 16)
    return {
        "currents": scatter_about(own_keys[0], (2, ANGLES, BOXES, UNK), 1.0, 6.0, ((1, 2), (2, 4))),
        "near_blocks": scatter_about(own_keys[1], (2, PAIRS, UNK, UNK), UNK ** -0.5, 0.375, ((1, 8),)),
        "near_pairs": draw_near_pairs(jax.random.fold_in(jax.random.fold_in(keys[15], part), 71), part),
        "near_count": draw_near_count(jax.random.fold_in(jax.random.fold_in(keys[15], part), 71), part),
        "radiation": scatter_about(own_keys[4], (2, BOXES, N_SUB, DIR0, UNK), UNK ** -0.5, 0.375, ((1, 4), (2, 2))),
        "parent_of": touch_ends(jax.random.randint(own_keys[5], (BOXES,), 0, PARENTS), jax.random.fold_in(own_keys[5], 1), 0, PARENTS - 1).astype(jnp.int32),
        "octant": touch_ends(jax.random.randint(own_keys[6], (BOXES,), 0, 8), jax.random.fold_in(own_keys[6], 1), 0, 7).astype(jnp.int32),
        "far0_src": touch_ends(jax.random.randint(own_keys[7], (BOXES, FAR0), 0, BOXES), jax.random.fold_in(own_keys[7], 1), 0, BOXES - 1).astype(jnp.int32),
        "far0_disp": touch_ends(jax.random.randint(own_keys[8], (BOXES, FAR0), 0, DISP), jax.random.fold_in(own_keys[8], 1), 0, DISP - 1).astype(jnp.int32),
        "far1_src": touch_ends(jax.random.randint(own_keys[9], (PARENTS, FAR1), 0, PARENTS), jax.random.fold_in(own_keys[9], 1), 0, PARENTS - 1).astype(jnp.int32),
        "far1_disp": touch_ends(jax.random.randint(own_keys[10], (PARENTS, FAR1), 0, DISP), jax.random.fold_in(own_keys[10], 1), 0, DISP - 1).astype(jnp.int32),
        "trans0": scatter_about(keys[11], (DISP, 2, DIR0), FAR0 ** -0.5, 1.5),
        "trans1": scatter_about(keys[12], (DISP, 2, DIR1), FAR1 ** -0.5, 2.0),
        "phases": jnp.clip(jax.random.uniform(keys[13], (8, DIR1), jnp.float32, -3.140625, 3.140625), -3.140625, 3.140625),
        "interp": scatter_about(keys[14], (DIR1, DIR0), DIR0 ** -0.5, 0.5, (), jnp.float32),
    }


def complex_times(left_real, left_imag, right_real, right_imag):
    return left_real * right_real - left_imag * right_imag, left_real * right_imag + left_imag * right_real


def translate_all(patterns, source_ids, kind_ids, op_table):
    table_wide = op_table.astype(jnp.float32)
    shape_out = (patterns.shape[0], patterns.shape[2], source_ids.shape[0], patterns.shape[4])
    total_real = jnp.zeros(shape_out, jnp.float32)
    total_imag = jnp.zeros(shape_out, jnp.float32)
    for column in range(source_ids.shape[1]):
        picked = patterns[:, :, :, source_ids[:, column]].astype(jnp.float32)
        coefficients = table_wide[kind_ids[:, column]]
        part_real, part_imag = complex_times(picked[:, 0], picked[:, 1], coefficients[:, 0], coefficients[:, 1])
        total_real = total_real + part_real
        total_imag = total_imag + part_imag
    return jnp.stack([total_real, total_imag], axis=1)


def reference(currents, near_blocks, near_pairs, near_count, radiation, parent_of, octant, far0_src, far0_disp, far1_src, far1_disp, trans0, trans1, phases, interp):
    highest = lax.Precision.HIGHEST

    def near_step(accumulated, pair_item):
        pair_block, pair_ids, slot_index = pair_item
        target = pair_ids[0]
        source = pair_ids[1]
        holder = slot_index // PAIR_DEV
        live_weight = ((slot_index % PAIR_DEV) < near_count[holder]).astype(jnp.float32)
        mirror_weight = live_weight * (target != source).astype(jnp.float32)
        block_real = pair_block[0]
        block_imag = pair_block[1]
        src_real = lax.dynamic_index_in_dim(currents[0], source, 1, False)
        src_imag = lax.dynamic_index_in_dim(currents[1], source, 1, False)
        tgt_real = lax.dynamic_index_in_dim(currents[0], target, 1, False)
        tgt_imag = lax.dynamic_index_in_dim(currents[1], target, 1, False)
        fwd_real = jnp.dot(src_real, block_real.T, preferred_element_type=jnp.float32) - jnp.dot(src_imag, block_imag.T, preferred_element_type=jnp.float32)
        fwd_imag = jnp.dot(src_real, block_imag.T, preferred_element_type=jnp.float32) + jnp.dot(src_imag, block_real.T, preferred_element_type=jnp.float32)
        back_real = jnp.dot(tgt_real, block_real, preferred_element_type=jnp.float32) - jnp.dot(tgt_imag, block_imag, preferred_element_type=jnp.float32)
        back_imag = jnp.dot(tgt_real, block_imag, preferred_element_type=jnp.float32) + jnp.dot(tgt_imag, block_real, preferred_element_type=jnp.float32)
        accumulated = accumulated.at[:, :, target].add(jnp.stack([fwd_real, fwd_imag]) * live_weight)
        accumulated = accumulated.at[:, :, source].add(jnp.stack([back_real, back_imag]) * mirror_weight)
        return accumulated, None

    blocks_major = jnp.moveaxis(near_blocks, 1, 0)
    start_field = jnp.zeros((2, ANGLES, BOXES, UNK), jnp.float32)
    near_field, _ = lax.scan(near_step, start_field, (blocks_major, near_pairs, jnp.arange(PAIRS, dtype=jnp.int32)))

    rad_wide = radiation.astype(jnp.float32)
    cur_wide = currents.astype(jnp.float32)
    pat_real = jnp.einsum("bqdu,abu->qabd", rad_wide[0], cur_wide[0], precision=highest) - jnp.einsum("bqdu,abu->qabd", rad_wide[1], cur_wide[1], precision=highest)
    pat_imag = jnp.einsum("bqdu,abu->qabd", rad_wide[0], cur_wide[1], precision=highest) + jnp.einsum("bqdu,abu->qabd", rad_wide[1], cur_wide[0], precision=highest)
    pattern = jnp.stack([pat_real, pat_imag], axis=1).astype(jnp.bfloat16)

    lifted_up = jnp.einsum("qcabd,ed->qcabe", pattern.astype(jnp.float32), interp, precision=highest)
    cosine = jnp.cos(phases[octant])
    sine_part = jnp.sin(phases[octant])
    lift_real, lift_imag = complex_times(lifted_up[:, 0], lifted_up[:, 1], cosine, sine_part)
    owner_map = (parent_of[None, :] == jnp.arange(PARENTS, dtype=jnp.int32)[:, None]).astype(jnp.float32)
    parent_real = jnp.einsum("rb,qabe->qare", owner_map, lift_real, precision=highest)
    parent_imag = jnp.einsum("rb,qabe->qare", owner_map, lift_imag, precision=highest)
    parent_pattern = jnp.stack([parent_real, parent_imag], axis=1).astype(jnp.bfloat16)
    parent_field = translate_all(parent_pattern, far1_src, far1_disp, trans1).astype(jnp.bfloat16)

    field_finest = translate_all(pattern, far0_src, far0_disp, trans0)
    from_parent = parent_field[:, :, :, parent_of].astype(jnp.float32)
    down_real, down_imag = complex_times(from_parent[:, 0], from_parent[:, 1], cosine, -sine_part)
    descended = jnp.einsum("qcabe,ed->qcabd", jnp.stack([down_real, down_imag], axis=1), interp, precision=highest)
    box_field = (field_finest + descended).astype(jnp.bfloat16)

    box_wide = box_field.astype(jnp.float32)
    far_real = jnp.einsum("bqdu,qabd->abu", rad_wide[0], box_wide[:, 0], precision=highest) - jnp.einsum("bqdu,qabd->abu", rad_wide[1], box_wide[:, 1], precision=highest)
    far_imag = jnp.einsum("bqdu,qabd->abu", rad_wide[0], box_wide[:, 1], precision=highest) + jnp.einsum("bqdu,qabd->abu", rad_wide[1], box_wide[:, 0], precision=highest)
    return (near_field + jnp.stack([far_real, far_imag])).astype(jnp.bfloat16)
```

```python
import functools

import jax
import jax.numpy as jnp
from jax import lax
from jax.experimental import pallas as pl
from jax.experimental.pallas import tpu as pltpu
from jax.sharding import PartitionSpec as P

BF16 = jnp.bfloat16
F32 = jnp.float32
MESH = pl.DeviceIdType.MESH


def turned(value):
    half = value.shape[0] // 2
    return jnp.concatenate([-value[half:], value[:half]], axis=0)


def dot(left, right, right_dim):
    return lax.dot_general(
        left, right, (((1,), (right_dim,)), ((), ())), preferred_element_type=F32
    )


def kernel(
    n,
    pairs,
    count,
    parent_of,
    octant,
    src0,
    disp0,
    src1,
    disp1,
    currents,
    near_blocks,
    radiation,
    trans0,
    trans1,
    phases,
    interp,
    out,
    staged,
    pool,
    pool_turned,
    blocks,
    rad,
    table0,
    table1,
    phase,
    cosine,
    sine,
    interp_wide,
    pattern,
    operators,
    lifted,
    parent,
    forward,
    backward,
    near_sum,
    mirror_out,
    mirror_in,
    half_out,
    half_in,
    local_sem,
    pattern_send,
    pattern_recv,
    operator_send,
    operator_recv,
    next_send,
    next_recv,
    mirror_send,
    mirror_recv,
    half_send,
    half_recv,
):
    me = lax.axis_index("box")
    sub = lax.axis_index("sub")
    slots = currents.shape[1]
    half_rows = currents.shape[2]
    rows = 2 * half_rows
    boxes = pattern.shape[0]
    parents = parent.shape[0]
    parents_here = src1.shape[0]
    slot_count = pairs.shape[1]
    own_start = me * slots

    own_pool = pool.at[pl.ds(0, slots)]
    next_pool = pool.at[pl.ds(slots, slots)]
    sources = (currents, radiation, phases, interp, trans1, near_blocks, trans0)
    targets = (staged, rad, phase, interp_wide, table1, blocks, table0)
    local = [
        pltpu.make_async_copy(a, b, local_sem.at[i])
        for i, (a, b) in enumerate(zip(sources, targets))
    ]
    for copy in local:
        copy.start()
    get_currents, get_rad, get_phase, get_interp, get_table1, get_blocks, get_table0 = local

    barrier = pltpu.get_barrier_semaphore()
    for step in range(1, n):
        pl.semaphore_signal(
            barrier, inc=1, device_id={"box": lax.rem(me + step, n)}, device_id_type=MESH
        )
    pl.semaphore_signal(barrier, inc=1, device_id={"sub": 1 - sub}, device_id_type=MESH)

    get_currents.wait()
    for b in range(slots):
        wide = jnp.concatenate([staged[0, b].astype(F32), staged[1, b].astype(F32)], axis=0)
        pool[b] = wide.astype(BF16)
        pool_turned[b] = turned(wide).astype(BF16)
    get_rad.wait()
    own_box = pl.ds(own_start, slots)
    for b in range(slots):
        pattern[own_start + b] = (
            dot(pool[b], rad[0, b, 0], 1) + dot(pool_turned[b], rad[1, b, 0], 1)
        ).astype(BF16)

    pl.semaphore_wait(barrier, n)

    pattern_copies = []
    for step in range(1, n):
        copy = pltpu.make_async_remote_copy(
            src_ref=pattern.at[own_box],
            dst_ref=pattern.at[own_box],
            send_sem=pattern_send.at[step - 1],
            recv_sem=pattern_recv.at[step - 1],
            device_id={"box": lax.rem(me + step, n)},
            device_id_type=MESH,
        )
        copy.start()
        pattern_copies.append(copy)

    next_copy = pltpu.make_async_remote_copy(
        src_ref=own_pool,
        dst_ref=next_pool,
        send_sem=next_send,
        recv_sem=next_recv,
        device_id={"box": lax.rem(me + n - 1, n)},
        device_id_type=MESH,
    )

    @pl.when(me > 0)
    def _():
        next_copy.start()

    @pl.when(me == n - 1)
    def _():
        pool[pl.ds(slots, slots)] = jnp.zeros((slots,) + pool.shape[1:], BF16)

    get_table1.wait()
    position = lax.broadcasted_iota(jnp.int32, (parents, table1.shape[2]), 0)
    own_operator = pl.ds(me * parents_here, parents_here)
    for r in range(parents_here):
        real = jnp.zeros(position.shape, F32)
        imag = jnp.zeros(position.shape, F32)
        for k in range(src1.shape[1]):
            row = table1[disp1[r, k]].astype(F32)
            hit = position == src1[r, k]
            real = real + jnp.where(hit, row[0:1], 0.0)
            imag = imag + jnp.where(hit, row[1:2], 0.0)
        operators[me * parents_here + r] = jnp.concatenate([real, imag], axis=0).astype(BF16)
    operator_copies = []
    for step in range(1, n):
        copy = pltpu.make_async_remote_copy(
            src_ref=operators.at[own_operator],
            dst_ref=operators.at[own_operator],
            send_sem=operator_send.at[step - 1],
            recv_sem=operator_recv.at[step - 1],
            device_id={"box": lax.rem(me + step, n)},
            device_id_type=MESH,
        )
        copy.start()
        operator_copies.append(copy)

    get_phase.wait()
    cosine[...] = jnp.cos(phase[...])
    sine[...] = jnp.sin(phase[...])

    @pl.when(me < n - 1)
    def _():
        next_copy.wait_recv()

    for b in range(slots, 2 * slots):
        pool_turned[b] = turned(pool[b].astype(F32)).astype(BF16)
    get_blocks.wait()

    def near_step(p, carry):
        source = jnp.clip(pairs[1, p] - own_start, 0, 2 * slots - 1)
        target = jnp.clip(pairs[0, p] - own_start, 0, slots - 1)
        forward[p] = dot(pool[source], blocks[0, p], 1) + dot(pool_turned[source], blocks[1, p], 1)
        backward[p] = dot(pool[target], blocks[0, p], 0) + dot(pool_turned[target], blocks[1, p], 0)
        return carry

    lax.fori_loop(0, slot_count, near_step, 0, unroll=True)

    def mirror_weight(p, b):
        source = pairs[1, p]
        hit = (source - own_start == b) & (source != pairs[0, p]) & (p < count[0])
        return jnp.where(hit, 1.0, 0.0).astype(F32)

    def target_weight(p, b):
        hit = (pairs[0, p] - own_start == b) & (p < count[0])
        return jnp.where(hit, 1.0, 0.0).astype(F32)

    zero = jnp.zeros(pool.shape[1:], F32)

    def mirror_box(b, carry):
        def step(p, total):
            return total + mirror_weight(p, slots + b) * backward[p]

        mirror_out[b] = lax.fori_loop(0, slot_count, step, zero, unroll=True).astype(BF16)
        return carry

    lax.fori_loop(0, slots, mirror_box, 0)
    mirror_copy = pltpu.make_async_remote_copy(
        src_ref=mirror_out,
        dst_ref=mirror_in,
        send_sem=mirror_send,
        recv_sem=mirror_recv,
        device_id={"box": lax.rem(me + 1, n)},
        device_id_type=MESH,
    )

    @pl.when(me < n - 1)
    def _():
        mirror_copy.start()

    @pl.when(me == 0)
    def _():
        mirror_in[...] = jnp.zeros(mirror_in.shape, BF16)

    def near_box(b, carry):
        def step(p, total):
            total = total + target_weight(p, b) * forward[p]
            return total + mirror_weight(p, b) * backward[p]

        near_sum[b] = lax.fori_loop(0, slot_count, step, zero, unroll=True)
        return carry

    lax.fori_loop(0, slots, near_box, 0)

    get_interp.wait()
    narrow = interp_wide[...].astype(BF16)
    for copy in pattern_copies:
        copy.wait_recv()

    def lift_box(b, carry):
        up = dot(pattern[b], narrow, 1)
        cos_row = cosine[pl.ds(octant[b], 1), :]
        sin_row = sine[pl.ds(octant[b], 1), :]
        real, imag = up[:half_rows], up[half_rows:]
        lifted[b] = jnp.concatenate(
            [real * cos_row - imag * sin_row, real * sin_row + imag * cos_row], axis=0
        )
        return carry

    def lift_some(part, carry):
        return lax.fori_loop(
            0, slots, lambda b, c: lift_box(part * slots + b, c), carry, unroll=True
        )

    lax.fori_loop(0, boxes // slots, lift_some, 0)

    def sum_parent(r, carry):
        def part_sum(part, total):
            def step(i, total):
                b = part * slots + i
                weight = jnp.where(parent_of[b] == r, 1.0, 0.0).astype(F32)
                return total + weight * lifted[b]

            return lax.fori_loop(0, slots, step, total, unroll=True)

        total = lax.fori_loop(0, boxes // slots, part_sum, zero)
        parent[r] = total.astype(BF16).astype(F32)
        return carry

    lax.fori_loop(0, parents, sum_parent, 0)

    for copy in operator_copies:
        copy.wait_recv()
    get_table0.wait()

    def far_box(b, carry):
        quarter = jnp.zeros((half_rows, pattern.shape[2]), F32)

        def translate(k, total):
            value = pattern[src0[b, k]].astype(F32)
            factor = table0[disp0[b, k]].astype(F32)
            real, imag = value[:half_rows], value[half_rows:]
            fr, fi = factor[0:1], factor[1:2]
            return (total[0] + (real * fr - imag * fi), total[1] + (real * fi + imag * fr))

        far_real, far_imag = lax.fori_loop(
            0, src0.shape[1], translate, (quarter, quarter), unroll=True
        )
        owner = parent_of[own_start + b]
        operator = operators[owner].astype(F32)
        pf_real = jnp.zeros((half_rows, parent.shape[2]), F32)
        pf_imag = jnp.zeros((half_rows, parent.shape[2]), F32)
        for s in range(parents):
            value = parent[s]
            real, imag = value[:half_rows], value[half_rows:]
            fr = operator[s : s + 1]
            fi = operator[parents + s : parents + s + 1]
            pf_real = pf_real + (real * fr - imag * fi)
            pf_imag = pf_imag + (real * fi + imag * fr)
        pf_real = pf_real.astype(BF16).astype(F32)
        pf_imag = pf_imag.astype(BF16).astype(F32)
        spot = octant[own_start + b]
        cos_row = cosine[pl.ds(spot, 1), :]
        sin_row = sine[pl.ds(spot, 1), :]
        down = jnp.concatenate(
            [pf_real * cos_row + pf_imag * sin_row, pf_imag * cos_row - pf_real * sin_row], axis=0
        ).astype(BF16)
        field = jnp.concatenate([far_real, far_imag], axis=0) + dot(down, narrow, 0)
        field = field.astype(BF16)
        wide = turned(field.astype(F32)).astype(BF16)
        near_sum[b] += dot(field, rad[0, b, 0], 0) + dot(wide, rad[1, b, 0], 0)
        return carry

    lax.fori_loop(0, slots, far_box, 0)

    @pl.when(me > 0)
    def _():
        mirror_copy.wait_recv()

    cut = out.shape[3]
    kept = []
    for b in range(slots):
        total = near_sum[b] + mirror_in[b].astype(F32)
        low, high = total[:, :cut], total[:, cut:]
        kept.append(jnp.where(sub == 0, low, high))
        half_out[b] = jnp.where(sub == 0, high, low).astype(BF16)
    half_copy = pltpu.make_async_remote_copy(
        src_ref=half_out,
        dst_ref=half_in,
        send_sem=half_send,
        recv_sem=half_recv,
        device_id={"sub": 1 - sub},
        device_id_type=MESH,
    )
    half_copy.start()
    for copy in pattern_copies + operator_copies:
        copy.wait_send()

    @pl.when(me > 0)
    def _():
        next_copy.wait_send()

    @pl.when(me < n - 1)
    def _():
        mirror_copy.wait_send()

    half_copy.wait()
    for b in range(slots):
        total = kept[b] + half_in[b].astype(F32)
        out[0, b] = total[:half_rows].astype(BF16)
        out[1, b] = total[half_rows:].astype(BF16)


def shards(
    n,
    currents,
    near_blocks,
    near_pairs,
    near_count,
    radiation,
    parent_of,
    octant,
    far0_src,
    far0_disp,
    far1_src,
    far1_disp,
    trans0,
    trans1,
    phases,
    interp,
):
    _, angles, slots, unknowns = currents.shape
    rows = 2 * angles
    boxes = parent_of.shape[0]
    parents_here = far1_src.shape[0]
    parents = n * parents_here
    fine, coarse = interp.shape[1], interp.shape[0]
    slot_count = near_pairs.shape[0]
    cut = unknowns // lax.axis_size("sub")
    per_box = jnp.transpose(currents, (0, 2, 1, 3))
    scalars = pl.BlockSpec(memory_space=pltpu.SMEM)
    away = pl.BlockSpec(memory_space=pl.ANY)
    dma = pltpu.SemaphoreType.DMA
    result = pl.pallas_call(
        functools.partial(kernel, n),
        out_shape=jax.ShapeDtypeStruct((2, slots, angles, cut), BF16),
        in_specs=[scalars] * 8 + [away] * 7,
        out_specs=pl.BlockSpec(memory_space=pltpu.VMEM),
        scratch_shapes=[
            pltpu.VMEM(per_box.shape, BF16),
            pltpu.VMEM((2 * slots, rows, unknowns), BF16),
            pltpu.VMEM((2 * slots, rows, unknowns), BF16),
            pltpu.VMEM(near_blocks.shape, BF16),
            pltpu.VMEM(radiation.shape, BF16),
            pltpu.VMEM(trans0.shape, BF16),
            pltpu.VMEM(trans1.shape, BF16),
            pltpu.VMEM(phases.shape, F32),
            pltpu.VMEM(phases.shape, F32),
            pltpu.VMEM(phases.shape, F32),
            pltpu.VMEM(interp.shape, F32),
            pltpu.VMEM((boxes, rows, fine), BF16),
            pltpu.VMEM((parents, 2 * parents, coarse), BF16),
            pltpu.VMEM((boxes, rows, coarse), F32),
            pltpu.VMEM((parents, rows, coarse), F32),
            pltpu.VMEM((slot_count, rows, unknowns), F32),
            pltpu.VMEM((slot_count, rows, unknowns), F32),
            pltpu.VMEM((slots, rows, unknowns), F32),
            pltpu.VMEM((slots, rows, unknowns), BF16),
            pltpu.VMEM((slots, rows, unknowns), BF16),
            pltpu.VMEM((slots, rows, cut), BF16),
            pltpu.VMEM((slots, rows, cut), BF16),
            dma((7,)),
            dma((n - 1,)),
            dma((n - 1,)),
            dma((n - 1,)),
            dma((n - 1,)),
            dma,
            dma,
            dma,
            dma,
            dma,
            dma,
        ],
        compiler_params=pltpu.CompilerParams(
            collective_id=0, has_side_effects=True, vmem_limit_bytes=60 * 1024 * 1024
        ),
    )(
        jnp.transpose(near_pairs),
        near_count,
        parent_of,
        octant,
        far0_src,
        far0_disp,
        far1_src,
        far1_disp,
        per_box,
        near_blocks,
        radiation,
        trans0,
        trans1,
        phases,
        interp,
    )
    return jnp.transpose(result, (0, 2, 1, 3))


def solution(mesh):
    placed = (
        P(None, "angle", ("groups", "box"), None),
        P(None, ("groups", "box", "sub"), None, None),
        P(("groups", "box", "sub"), None),
        P(("groups", "box", "sub")),
        P(None, ("groups", "box"), "sub", None, None),
        P("groups"),
        P("groups"),
        P(("groups", "box"), None),
        P(("groups", "box"), None),
        P(("groups", "box"), None),
        P(("groups", "box"), None),
        P(),
        P(),
        P(),
        P(),
    )
    return jax.shard_map(
        functools.partial(shards, mesh.shape["box"]),
        mesh=mesh,
        in_specs=placed,
        out_specs=P(None, "angle", ("groups", "box"), "sub"),
        check_vma=False,
    )
```

```python
import functools

import jax
import jax.numpy as jnp
from jax import lax
from jax.experimental import pallas as pl
from jax.experimental.pallas import tpu as pltpu
from jax.sharding import PartitionSpec as P

BF16 = jnp.bfloat16
F32 = jnp.float32
MESH = pl.DeviceIdType.MESH


def turned(value):
    half = value.shape[0] // 2
    return jnp.concatenate([-value[half:], value[:half]], axis=0)


def dot(left, right, right_dim):
    return lax.dot_general(
        left, right, (((1,), (right_dim,)), ((), ())), preferred_element_type=F32
    )


def kernel(
    n,
    pairs_hbm,
    count_hbm,
    parent_of_hbm,
    octant_hbm,
    src0_hbm,
    disp0_hbm,
    src1_hbm,
    disp1_hbm,
    currents,
    near_blocks,
    radiation,
    trans0,
    trans1,
    phases,
    interp,
    out,
    pairs,
    count,
    parent_of,
    octant,
    src0,
    disp0,
    src1,
    disp1,
    staged,
    pool,
    pool_turned,
    blocks,
    rad,
    table0,
    table1,
    phase,
    cosine,
    sine,
    interp_wide,
    pattern,
    operators,
    lifted,
    parent,
    forward,
    backward,
    near_sum,
    mirror_out,
    mirror_in,
    half_out,
    half_in,
    local_sem,
    pattern_send,
    pattern_recv,
    operator_send,
    operator_recv,
    next_send,
    next_recv,
    mirror_send,
    mirror_recv,
    half_send,
    half_recv,
):
    me = lax.axis_index("box")
    sub = lax.axis_index("sub")
    slots = currents.shape[1]
    half_rows = currents.shape[2]
    rows = 2 * half_rows
    boxes = pattern.shape[0]
    parents = parent.shape[0]
    parents_here = src1.shape[0]
    slot_count = pairs.shape[1]
    own_start = me * slots

    barrier = pltpu.get_barrier_semaphore()
    for step in range(1, n):
        pl.semaphore_signal(
            barrier, inc=1, device_id={"box": lax.rem(me + step, n)}, device_id_type=MESH
        )
    pl.semaphore_signal(barrier, inc=1, device_id={"sub": 1 - sub}, device_id_type=MESH)

    own_pool = pool.at[pl.ds(0, slots)]
    next_pool = pool.at[pl.ds(slots, slots)]
    sources = (
        currents,
        radiation,
        disp1_hbm,
        src1_hbm,
        trans1,
        phases,
        octant_hbm,
        parent_of_hbm,
        src0_hbm,
        disp0_hbm,
        pairs_hbm,
        count_hbm,
        interp,
        trans0,
        near_blocks,
    )
    targets = (
        staged,
        rad,
        disp1,
        src1,
        table1,
        phase,
        octant,
        parent_of,
        src0,
        disp0,
        pairs,
        count,
        interp_wide,
        table0,
        blocks,
    )
    local = [
        pltpu.make_async_copy(a, b, local_sem.at[i])
        for i, (a, b) in enumerate(zip(sources, targets))
    ]
    for copy in local:
        copy.start()
    get_currents, get_rad, *get_parent_lists = local[:5]
    get_phase, *get_lists = local[5:12]
    get_interp, get_table0, get_blocks = local[12:]

    get_currents.wait()
    for b in range(slots):
        wide = jnp.concatenate([staged[0, b].astype(F32), staged[1, b].astype(F32)], axis=0)
        pool[b] = wide.astype(BF16)
        pool_turned[b] = turned(wide).astype(BF16)
    get_rad.wait()
    own_box = pl.ds(own_start, slots)
    for b in range(slots):
        pattern[own_start + b] = (
            dot(pool[b], rad[0, b, 0], 1) + dot(pool_turned[b], rad[1, b, 0], 1)
        ).astype(BF16)

    pl.semaphore_wait(barrier, n)

    pattern_copies = []
    for step in range(1, n):
        copy = pltpu.make_async_remote_copy(
            src_ref=pattern.at[own_box],
            dst_ref=pattern.at[own_box],
            send_sem=pattern_send.at[step - 1],
            recv_sem=pattern_recv.at[step - 1],
            device_id={"box": lax.rem(me + step, n)},
            device_id_type=MESH,
        )
        copy.start()
        pattern_copies.append(copy)

    next_copy = pltpu.make_async_remote_copy(
        src_ref=own_pool,
        dst_ref=next_pool,
        send_sem=next_send,
        recv_sem=next_recv,
        device_id={"box": lax.rem(me + n - 1, n)},
        device_id_type=MESH,
    )

    @pl.when(me > 0)
    def _():
        next_copy.start()

    @pl.when(me == n - 1)
    def _():
        pool[pl.ds(slots, slots)] = jnp.zeros((slots,) + pool.shape[1:], BF16)

    for copy in get_parent_lists:
        copy.wait()
    position = lax.broadcasted_iota(jnp.int32, (parents, table1.shape[2]), 0)
    own_operator = pl.ds(me * parents_here, parents_here)
    for r in range(parents_here):
        real = jnp.zeros(position.shape, F32)
        imag = jnp.zeros(position.shape, F32)
        for k in range(src1.shape[1]):
            row = table1[disp1[r, k]].astype(F32)
            hit = position == src1[r, k]
            real = real + jnp.where(hit, row[0:1], 0.0)
            imag = imag + jnp.where(hit, row[1:2], 0.0)
        operators[me * parents_here + r] = jnp.concatenate([real, imag], axis=0).astype(BF16)
    operator_copies = []
    for step in range(1, n):
        copy = pltpu.make_async_remote_copy(
            src_ref=operators.at[own_operator],
            dst_ref=operators.at[own_operator],
            send_sem=operator_send.at[step - 1],
            recv_sem=operator_recv.at[step - 1],
            device_id={"box": lax.rem(me + step, n)},
            device_id_type=MESH,
        )
        copy.start()
        operator_copies.append(copy)

    get_phase.wait()
    cosine[...] = jnp.cos(phase[...])
    sine[...] = jnp.sin(phase[...])

    @pl.when(me < n - 1)
    def _():
        next_copy.wait_recv()

    for b in range(slots, 2 * slots):
        pool_turned[b] = turned(pool[b].astype(F32)).astype(BF16)
    for copy in get_lists:
        copy.wait()
    get_blocks.wait()

    def near_step(p, carry):
        source = jnp.clip(pairs[1, p] - own_start, 0, 2 * slots - 1)
        target = jnp.clip(pairs[0, p] - own_start, 0, slots - 1)
        forward[p] = dot(pool[source], blocks[0, p], 1) + dot(pool_turned[source], blocks[1, p], 1)
        backward[p] = dot(pool[target], blocks[0, p], 0) + dot(pool_turned[target], blocks[1, p], 0)
        return carry

    lax.fori_loop(0, slot_count, near_step, 0, unroll=True)

    def mirror_weight(p, b):
        source = pairs[1, p]
        hit = (source - own_start == b) & (source != pairs[0, p]) & (p < count[0])
        return jnp.where(hit, 1.0, 0.0).astype(F32)

    def target_weight(p, b):
        hit = (pairs[0, p] - own_start == b) & (p < count[0])
        return jnp.where(hit, 1.0, 0.0).astype(F32)

    zero = jnp.zeros(pool.shape[1:], F32)

    def mirror_box(b, carry):
        def step(p, total):
            return total + mirror_weight(p, slots + b) * backward[p]

        mirror_out[b] = lax.fori_loop(0, slot_count, step, zero, unroll=True).astype(BF16)
        return carry

    lax.fori_loop(0, slots, mirror_box, 0)
    mirror_copy = pltpu.make_async_remote_copy(
        src_ref=mirror_out,
        dst_ref=mirror_in,
        send_sem=mirror_send,
        recv_sem=mirror_recv,
        device_id={"box": lax.rem(me + 1, n)},
        device_id_type=MESH,
    )

    @pl.when(me < n - 1)
    def _():
        mirror_copy.start()

    @pl.when(me == 0)
    def _():
        mirror_in[...] = jnp.zeros(mirror_in.shape, BF16)

    def near_box(b, carry):
        def step(p, total):
            total = total + target_weight(p, b) * forward[p]
            return total + mirror_weight(p, b) * backward[p]

        near_sum[b] = lax.fori_loop(0, slot_count, step, zero, unroll=True)
        return carry

    lax.fori_loop(0, slots, near_box, 0)

    get_interp.wait()
    narrow = interp_wide[...].astype(BF16)
    for copy in pattern_copies:
        copy.wait_recv()

    def lift_box(b, carry):
        up = dot(pattern[b], narrow, 1)
        cos_row = cosine[pl.ds(octant[b], 1), :]
        sin_row = sine[pl.ds(octant[b], 1), :]
        real, imag = up[:half_rows], up[half_rows:]
        lifted[b] = jnp.concatenate(
            [real * cos_row - imag * sin_row, real * sin_row + imag * cos_row], axis=0
        )
        return carry

    def lift_some(part, carry):
        return lax.fori_loop(
            0, slots, lambda b, c: lift_box(part * slots + b, c), carry, unroll=True
        )

    lax.fori_loop(0, boxes // slots, lift_some, 0)

    def sum_parent(r, carry):
        def part_sum(part, total):
            def step(i, total):
                b = part * slots + i
                weight = jnp.where(parent_of[b] == r, 1.0, 0.0).astype(F32)
                return total + weight * lifted[b]

            return lax.fori_loop(0, slots, step, total, unroll=True)

        total = lax.fori_loop(0, boxes // slots, part_sum, zero)
        parent[r] = total.astype(BF16).astype(F32)
        return carry

    lax.fori_loop(0, parents, sum_parent, 0)

    for copy in operator_copies:
        copy.wait_recv()
    get_table0.wait()

    def far_box(b, carry):
        quarter = jnp.zeros((half_rows, pattern.shape[2]), F32)

        def translate(k, total):
            value = pattern[src0[b, k]].astype(F32)
            factor = table0[disp0[b, k]].astype(F32)
            real, imag = value[:half_rows], value[half_rows:]
            fr, fi = factor[0:1], factor[1:2]
            return (total[0] + (real * fr - imag * fi), total[1] + (real * fi + imag * fr))

        far_real, far_imag = lax.fori_loop(
            0, src0.shape[1], translate, (quarter, quarter), unroll=True
        )
        owner = parent_of[own_start + b]
        operator = operators[owner].astype(F32)
        pf_real = jnp.zeros((half_rows, parent.shape[2]), F32)
        pf_imag = jnp.zeros((half_rows, parent.shape[2]), F32)
        for s in range(parents):
            value = parent[s]
            real, imag = value[:half_rows], value[half_rows:]
            fr = operator[s : s + 1]
            fi = operator[parents + s : parents + s + 1]
            pf_real = pf_real + (real * fr - imag * fi)
            pf_imag = pf_imag + (real * fi + imag * fr)
        pf_real = pf_real.astype(BF16).astype(F32)
        pf_imag = pf_imag.astype(BF16).astype(F32)
        spot = octant[own_start + b]
        cos_row = cosine[pl.ds(spot, 1), :]
        sin_row = sine[pl.ds(spot, 1), :]
        down = jnp.concatenate(
            [pf_real * cos_row + pf_imag * sin_row, pf_imag * cos_row - pf_real * sin_row], axis=0
        ).astype(BF16)
        field = jnp.concatenate([far_real, far_imag], axis=0) + dot(down, narrow, 0)
        field = field.astype(BF16)
        wide = turned(field.astype(F32)).astype(BF16)
        near_sum[b] += dot(field, rad[0, b, 0], 0) + dot(wide, rad[1, b, 0], 0)
        return carry

    lax.fori_loop(0, slots, far_box, 0)

    @pl.when(me > 0)
    def _():
        mirror_copy.wait_recv()

    cut = out.shape[3]
    kept = []
    for b in range(slots):
        total = near_sum[b] + mirror_in[b].astype(F32)
        low, high = total[:, :cut], total[:, cut:]
        kept.append(jnp.where(sub == 0, low, high))
        half_out[b] = jnp.where(sub == 0, high, low).astype(BF16)
    half_copy = pltpu.make_async_remote_copy(
        src_ref=half_out,
        dst_ref=half_in,
        send_sem=half_send,
        recv_sem=half_recv,
        device_id={"sub": 1 - sub},
        device_id_type=MESH,
    )
    half_copy.start()
    for copy in pattern_copies + operator_copies:
        copy.wait_send()

    @pl.when(me > 0)
    def _():
        next_copy.wait_send()

    @pl.when(me < n - 1)
    def _():
        mirror_copy.wait_send()

    half_copy.wait()
    for b in range(slots):
        total = kept[b] + half_in[b].astype(F32)
        out[0, b] = total[:half_rows].astype(BF16)
        out[1, b] = total[half_rows:].astype(BF16)


def shards(
    n,
    currents,
    near_blocks,
    near_pairs,
    near_count,
    radiation,
    parent_of,
    octant,
    far0_src,
    far0_disp,
    far1_src,
    far1_disp,
    trans0,
    trans1,
    phases,
    interp,
):
    _, angles, slots, unknowns = currents.shape
    rows = 2 * angles
    boxes = parent_of.shape[0]
    parents_here = far1_src.shape[0]
    parents = n * parents_here
    fine, coarse = interp.shape[1], interp.shape[0]
    slot_count = near_pairs.shape[0]
    cut = unknowns // lax.axis_size("sub")
    per_box = jnp.transpose(currents, (0, 2, 1, 3))
    away = pl.BlockSpec(memory_space=pltpu.HBM)
    lists = (near_pairs.T, near_count, parent_of, octant, far0_src, far0_disp, far1_src, far1_disp)
    dma = pltpu.SemaphoreType.DMA
    result = pl.pallas_call(
        functools.partial(kernel, n),
        out_shape=jax.ShapeDtypeStruct((2, slots, angles, cut), BF16),
        in_specs=[away] * 15,
        out_specs=pl.BlockSpec(memory_space=pltpu.VMEM),
        scratch_shapes=[pltpu.SMEM(entry.shape, jnp.int32) for entry in lists]
        + [
            pltpu.VMEM(per_box.shape, BF16),
            pltpu.VMEM((2 * slots, rows, unknowns), BF16),
            pltpu.VMEM((2 * slots, rows, unknowns), BF16),
            pltpu.VMEM(near_blocks.shape, BF16),
            pltpu.VMEM(radiation.shape, BF16),
            pltpu.VMEM(trans0.shape, BF16),
            pltpu.VMEM(trans1.shape, BF16),
            pltpu.VMEM(phases.shape, F32),
            pltpu.VMEM(phases.shape, F32),
            pltpu.VMEM(phases.shape, F32),
            pltpu.VMEM(interp.shape, F32),
            pltpu.VMEM((boxes, rows, fine), BF16),
            pltpu.VMEM((parents, 2 * parents, coarse), BF16),
            pltpu.VMEM((boxes, rows, coarse), F32),
            pltpu.VMEM((parents, rows, coarse), F32),
            pltpu.VMEM((slot_count, rows, unknowns), F32),
            pltpu.VMEM((slot_count, rows, unknowns), F32),
            pltpu.VMEM((slots, rows, unknowns), F32),
            pltpu.VMEM((slots, rows, unknowns), BF16),
            pltpu.VMEM((slots, rows, unknowns), BF16),
            pltpu.VMEM((slots, rows, cut), BF16),
            pltpu.VMEM((slots, rows, cut), BF16),
            dma((15,)),
            dma((n - 1,)),
            dma((n - 1,)),
            dma((n - 1,)),
            dma((n - 1,)),
            dma,
            dma,
            dma,
            dma,
            dma,
            dma,
        ],
        compiler_params=pltpu.CompilerParams(
            collective_id=0, has_side_effects=True, vmem_limit_bytes=60 * 1024 * 1024
        ),
    )(
        *lists,
        per_box,
        near_blocks,
        radiation,
        trans0,
        trans1,
        phases,
        interp,
    )
    return jnp.transpose(result, (0, 2, 1, 3))


def solution(mesh):
    placed = (
        P(None, "angle", ("groups", "box"), None),
        P(None, ("groups", "box", "sub"), None, None),
        P(("groups", "box", "sub"), None),
        P(("groups", "box", "sub")),
        P(None, ("groups", "box"), "sub", None, None),
        P("groups"),
        P("groups"),
        P(("groups", "box"), None),
        P(("groups", "box"), None),
        P(("groups", "box"), None),
        P(("groups", "box"), None),
        P(),
        P(),
        P(),
        P(),
    )
    return jax.shard_map(
        functools.partial(shards, mesh.shape["box"]),
        mesh=mesh,
        in_specs=placed,
        out_specs=P(None, "angle", ("groups", "box"), "sub"),
        check_vma=False,
    )
```

```python
import functools

import jax
import jax.numpy as jnp
from jax import lax
from jax.experimental import pallas as pl
from jax.experimental.pallas import tpu as pltpu
from jax.sharding import PartitionSpec as P

BF16 = jnp.bfloat16
F32 = jnp.float32
MESH = pl.DeviceIdType.MESH


def turned(value):
    half = value.shape[0] // 2
    return jnp.concatenate([-value[half:], value[:half]], axis=0)


def dot(left, right, right_dim):
    return lax.dot_general(
        left, right, (((1,), (right_dim,)), ((), ())), preferred_element_type=F32
    )


def kernel(
    n,
    pairs_hbm,
    count_hbm,
    parent_of_hbm,
    octant_hbm,
    src0_hbm,
    disp0_hbm,
    src1_hbm,
    disp1_hbm,
    currents,
    near_blocks,
    radiation,
    trans0,
    trans1,
    phases,
    interp,
    out,
    pairs,
    count,
    parent_of,
    octant,
    src0,
    disp0,
    src1,
    disp1,
    staged,
    mine,
    pool,
    pool_turned,
    blocks,
    rad,
    table0,
    table1,
    phase,
    cosine,
    sine,
    interp_wide,
    pattern,
    operators,
    lifted,
    down,
    parent,
    forward,
    backward,
    near_sum,
    mirror_out,
    mirror_in,
    half_out,
    half_in,
    local_sem,
    pattern_send,
    pattern_recv,
    operator_send,
    operator_recv,
    next_send,
    next_recv,
    mirror_send,
    mirror_recv,
    half_send,
    half_recv,
):
    me = lax.axis_index("box")
    sub = lax.axis_index("sub")
    slots = currents.shape[1]
    half_rows = currents.shape[2]
    rows = 2 * half_rows
    boxes = pattern.shape[0]
    parents = parent.shape[0]
    parents_here = src1.shape[0]
    slot_count = pairs.shape[1]
    own_start = me * slots

    barrier = pltpu.get_barrier_semaphore()
    for step in range(1, n):
        pl.semaphore_signal(
            barrier, inc=1, device_id={"box": lax.rem(me + step, n)}, device_id_type=MESH
        )
    pl.semaphore_signal(barrier, inc=1, device_id={"sub": 1 - sub}, device_id_type=MESH)

    next_pool = pool.at[pl.ds(slots, slots)]
    sources = (
        currents,
        radiation,
        disp1_hbm,
        src1_hbm,
        trans1,
        phases,
        octant_hbm,
        parent_of_hbm,
        src0_hbm,
        disp0_hbm,
        pairs_hbm,
        count_hbm,
        interp,
        trans0,
        near_blocks,
    )
    targets = (
        staged,
        rad,
        disp1,
        src1,
        table1,
        phase,
        octant,
        parent_of,
        src0,
        disp0,
        pairs,
        count,
        interp_wide,
        table0,
        blocks,
    )
    local = [
        pltpu.make_async_copy(a, b, local_sem.at[i])
        for i, (a, b) in enumerate(zip(sources, targets))
    ]
    for copy in local[:-1]:
        copy.start()
    get_currents, get_rad, *get_parent_lists = local[:5]
    get_phase, *get_lists = local[5:12]
    get_interp, get_table0, get_blocks = local[12:]

    get_currents.wait()
    for b in range(slots):
        wide = jnp.concatenate([staged[0, b].astype(F32), staged[1, b].astype(F32)], axis=0)
        mine[b] = wide.astype(BF16)
        pool[b] = wide.astype(BF16)
        pool_turned[b] = turned(wide).astype(BF16)
    get_rad.wait()
    get_blocks.start()
    own_box = pl.ds(own_start, slots)
    for b in range(slots):
        pattern[own_start + b] = (
            dot(mine[b], rad[0, b, 0], 1) + dot(pool_turned[b], rad[1, b, 0], 1)
        ).astype(BF16)

    pl.semaphore_wait(barrier, n)

    pattern_copies = []
    for step in range(1, n):
        copy = pltpu.make_async_remote_copy(
            src_ref=pattern.at[own_box],
            dst_ref=pattern.at[own_box],
            send_sem=pattern_send.at[step - 1],
            recv_sem=pattern_recv.at[step - 1],
            device_id={"box": lax.rem(me + step, n)},
            device_id_type=MESH,
        )
        copy.start()
        pattern_copies.append(copy)

    next_copy = pltpu.make_async_remote_copy(
        src_ref=mine,
        dst_ref=next_pool,
        send_sem=next_send,
        recv_sem=next_recv,
        device_id={"box": lax.rem(me + n - 1, n)},
        device_id_type=MESH,
    )

    @pl.when(me > 0)
    def _():
        next_copy.start()

    @pl.when(me == n - 1)
    def _():
        pool[pl.ds(slots, slots)] = jnp.zeros((slots,) + pool.shape[1:], BF16)

    for copy in get_parent_lists:
        copy.wait()
    position = lax.broadcasted_iota(jnp.int32, (parents, table1.shape[2]), 0)
    own_operator = pl.ds(me * parents_here, parents_here)
    for r in range(parents_here):
        real = jnp.zeros(position.shape, F32)
        imag = jnp.zeros(position.shape, F32)
        for k in range(src1.shape[1]):
            row = table1[disp1[r, k]].astype(F32)
            hit = position == src1[r, k]
            real = real + jnp.where(hit, row[0:1], 0.0)
            imag = imag + jnp.where(hit, row[1:2], 0.0)
        operators[me * parents_here + r] = jnp.concatenate([real, imag], axis=0).astype(BF16)
    operator_copies = []
    for step in range(1, n):
        copy = pltpu.make_async_remote_copy(
            src_ref=operators.at[own_operator],
            dst_ref=operators.at[own_operator],
            send_sem=operator_send.at[step - 1],
            recv_sem=operator_recv.at[step - 1],
            device_id={"box": lax.rem(me + step, n)},
            device_id_type=MESH,
        )
        copy.start()
        operator_copies.append(copy)

    for copy in get_lists:
        copy.wait()
    get_blocks.wait()

    def backward_step(p, carry):
        target = jnp.clip(pairs[0, p] - own_start, 0, slots - 1)
        backward[p] = dot(mine[target], blocks[0, p], 0) + dot(pool_turned[target], blocks[1, p], 0)
        return carry

    lax.fori_loop(0, slot_count, backward_step, 0, unroll=True)

    def mirror_weight(p, b):
        source = pairs[1, p]
        hit = (source - own_start == b) & (source != pairs[0, p]) & (p < count[0])
        return jnp.where(hit, 1.0, 0.0).astype(F32)

    def target_weight(p, b):
        hit = (pairs[0, p] - own_start == b) & (p < count[0])
        return jnp.where(hit, 1.0, 0.0).astype(F32)

    zero = jnp.zeros(pool.shape[1:], F32)

    def mirror_box(b, carry):
        def step(p, total):
            return total + mirror_weight(p, slots + b) * backward[p]

        mirror_out[b] = lax.fori_loop(0, slot_count, step, zero, unroll=True).astype(BF16)
        return carry

    lax.fori_loop(0, slots, mirror_box, 0)
    mirror_copy = pltpu.make_async_remote_copy(
        src_ref=mirror_out,
        dst_ref=mirror_in,
        send_sem=mirror_send,
        recv_sem=mirror_recv,
        device_id={"box": lax.rem(me + 1, n)},
        device_id_type=MESH,
    )

    @pl.when(me < n - 1)
    def _():
        mirror_copy.start()

    @pl.when(me == 0)
    def _():
        mirror_in[...] = jnp.zeros(mirror_in.shape, BF16)

    get_phase.wait()
    cosine[...] = jnp.cos(phase[...])
    sine[...] = jnp.sin(phase[...])
    get_interp.wait()
    narrow = interp_wide[...].astype(BF16)
    parent[...] = jnp.zeros(parent.shape, F32)
    merged = slots * rows

    def lift_part(part):
        start = part * slots
        part_rows = pattern[pl.ds(start, slots)].reshape(merged, pattern.shape[2])
        up = dot(part_rows, narrow, 1)
        for i in range(slots):
            cos_row = cosine[pl.ds(octant[start + i], 1), :]
            sin_row = sine[pl.ds(octant[start + i], 1), :]
            real = up[i * rows : i * rows + half_rows]
            imag = up[i * rows + half_rows : (i + 1) * rows]
            lifted[i] = jnp.concatenate(
                [real * cos_row - imag * sin_row, real * sin_row + imag * cos_row], axis=0
            )

        def sum_parent(r, carry):
            total = parent[r]
            for i in range(slots):
                weight = jnp.where(parent_of[start + i] == r, 1.0, 0.0).astype(F32)
                total = total + weight * lifted[i]
            parent[r] = total
            return carry

        lax.fori_loop(0, parents, sum_parent, 0, unroll=parents <= 8)

    lift_part(me)

    @pl.when(me < n - 1)
    def _():
        next_copy.wait_recv()

    for b in range(slots, 2 * slots):
        pool_turned[b] = turned(pool[b].astype(F32)).astype(BF16)

    def forward_step(p, carry):
        source = jnp.clip(pairs[1, p] - own_start, 0, 2 * slots - 1)
        forward[p] = dot(pool[source], blocks[0, p], 1) + dot(pool_turned[source], blocks[1, p], 1)
        return carry

    lax.fori_loop(0, slot_count, forward_step, 0, unroll=True)

    def near_box(b, carry):
        def step(p, total):
            total = total + target_weight(p, b) * forward[p]
            return total + mirror_weight(p, b) * backward[p]

        near_sum[b] = lax.fori_loop(0, slot_count, step, zero, unroll=True)
        return carry

    lax.fori_loop(0, slots, near_box, 0)

    for step in sorted(range(1, n), key=lambda k: min(k, n - k)):
        pattern_copies[step - 1].wait_recv()
        lift_part(lax.rem(me + n - step, n))

    for copy in operator_copies:
        copy.wait_recv()
    get_table0.wait()

    def round_parent(r, carry):
        parent[r] = parent[r].astype(BF16).astype(F32)
        return carry

    lax.fori_loop(0, parents, round_parent, 0, unroll=parents <= 8)

    for b in range(slots):
        owner = parent_of[own_start + b]
        pf_real = jnp.zeros((half_rows, parent.shape[2]), F32)
        pf_imag = jnp.zeros((half_rows, parent.shape[2]), F32)
        operator = operators[owner].astype(F32)
        for s in range(parents):
            value = parent[s]
            real, imag = value[:half_rows], value[half_rows:]
            fr = operator[s : s + 1]
            fi = operator[parents + s : parents + s + 1]
            pf_real = pf_real + (real * fr - imag * fi)
            pf_imag = pf_imag + (real * fi + imag * fr)
        pf_real = pf_real.astype(BF16).astype(F32)
        pf_imag = pf_imag.astype(BF16).astype(F32)
        spot = octant[own_start + b]
        cos_row = cosine[pl.ds(spot, 1), :]
        sin_row = sine[pl.ds(spot, 1), :]
        down[b] = jnp.concatenate(
            [pf_real * cos_row + pf_imag * sin_row, pf_imag * cos_row - pf_real * sin_row], axis=0
        ).astype(BF16)
    descended = dot(down[...].reshape(merged, down.shape[2]), narrow, 0)

    quarter = jnp.zeros((half_rows, pattern.shape[2]), F32)
    for b in range(slots):

        def translate(k, total):
            value = pattern[src0[b, k]].astype(F32)
            factor = table0[disp0[b, k]].astype(F32)
            real, imag = value[:half_rows], value[half_rows:]
            fr, fi = factor[0:1], factor[1:2]
            return (total[0] + (real * fr - imag * fi), total[1] + (real * fi + imag * fr))

        far_real, far_imag = lax.fori_loop(
            0, src0.shape[1], translate, (quarter, quarter), unroll=True
        )
        field = jnp.concatenate([far_real, far_imag], axis=0) + descended[b * rows : (b + 1) * rows]
        field = field.astype(BF16)
        wide = turned(field.astype(F32)).astype(BF16)
        near_sum[b] += dot(field, rad[0, b, 0], 0) + dot(wide, rad[1, b, 0], 0)

    @pl.when(me > 0)
    def _():
        mirror_copy.wait_recv()

    cut = out.shape[3]
    kept = []
    for b in range(slots):
        total = near_sum[b] + mirror_in[b].astype(F32)
        low, high = total[:, :cut], total[:, cut:]
        kept.append(jnp.where(sub == 0, low, high))
        half_out[b] = jnp.where(sub == 0, high, low).astype(BF16)
    half_copy = pltpu.make_async_remote_copy(
        src_ref=half_out,
        dst_ref=half_in,
        send_sem=half_send,
        recv_sem=half_recv,
        device_id={"sub": 1 - sub},
        device_id_type=MESH,
    )
    half_copy.start()
    for copy in pattern_copies + operator_copies:
        copy.wait_send()

    @pl.when(me > 0)
    def _():
        next_copy.wait_send()

    @pl.when(me < n - 1)
    def _():
        mirror_copy.wait_send()

    half_copy.wait()
    for b in range(slots):
        total = kept[b] + half_in[b].astype(F32)
        out[0, b] = total[:half_rows].astype(BF16)
        out[1, b] = total[half_rows:].astype(BF16)


def shards(
    n,
    currents,
    near_blocks,
    near_pairs,
    near_count,
    radiation,
    parent_of,
    octant,
    far0_src,
    far0_disp,
    far1_src,
    far1_disp,
    trans0,
    trans1,
    phases,
    interp,
):
    _, angles, slots, unknowns = currents.shape
    rows = 2 * angles
    boxes = parent_of.shape[0]
    parents_here = far1_src.shape[0]
    parents = n * parents_here
    fine, coarse = interp.shape[1], interp.shape[0]
    slot_count = near_pairs.shape[0]
    cut = unknowns // lax.axis_size("sub")
    per_box = jnp.transpose(currents, (0, 2, 1, 3))
    away = pl.BlockSpec(memory_space=pltpu.HBM)
    lists = (near_pairs.T, near_count, parent_of, octant, far0_src, far0_disp, far1_src, far1_disp)
    dma = pltpu.SemaphoreType.DMA
    result = pl.pallas_call(
        functools.partial(kernel, n),
        out_shape=jax.ShapeDtypeStruct((2, slots, angles, cut), BF16),
        in_specs=[away] * 15,
        out_specs=pl.BlockSpec(memory_space=pltpu.VMEM),
        scratch_shapes=[pltpu.SMEM(entry.shape, jnp.int32) for entry in lists]
        + [
            pltpu.VMEM(per_box.shape, BF16),
            pltpu.VMEM((slots, rows, unknowns), BF16),
            pltpu.VMEM((2 * slots, rows, unknowns), BF16),
            pltpu.VMEM((2 * slots, rows, unknowns), BF16),
            pltpu.VMEM(near_blocks.shape, BF16),
            pltpu.VMEM(radiation.shape, BF16),
            pltpu.VMEM(trans0.shape, BF16),
            pltpu.VMEM(trans1.shape, BF16),
            pltpu.VMEM(phases.shape, F32),
            pltpu.VMEM(phases.shape, F32),
            pltpu.VMEM(phases.shape, F32),
            pltpu.VMEM(interp.shape, F32),
            pltpu.VMEM((boxes, rows, fine), BF16),
            pltpu.VMEM((parents, 2 * parents, coarse), BF16),
            pltpu.VMEM((slots, rows, coarse), F32),
            pltpu.VMEM((slots, rows, coarse), BF16),
            pltpu.VMEM((parents, rows, coarse), F32),
            pltpu.VMEM((slot_count, rows, unknowns), F32),
            pltpu.VMEM((slot_count, rows, unknowns), F32),
            pltpu.VMEM((slots, rows, unknowns), F32),
            pltpu.VMEM((slots, rows, unknowns), BF16),
            pltpu.VMEM((slots, rows, unknowns), BF16),
            pltpu.VMEM((slots, rows, cut), BF16),
            pltpu.VMEM((slots, rows, cut), BF16),
            dma((15,)),
            dma((n - 1,)),
            dma((n - 1,)),
            dma((n - 1,)),
            dma((n - 1,)),
            dma,
            dma,
            dma,
            dma,
            dma,
            dma,
        ],
        compiler_params=pltpu.CompilerParams(
            collective_id=0, has_side_effects=True, vmem_limit_bytes=60 * 1024 * 1024
        ),
    )(
        *lists,
        per_box,
        near_blocks,
        radiation,
        trans0,
        trans1,
        phases,
        interp,
    )
    return jnp.transpose(result, (0, 2, 1, 3))


def solution(mesh):
    placed = (
        P(None, "angle", ("groups", "box"), None),
        P(None, ("groups", "box", "sub"), None, None),
        P(("groups", "box", "sub"), None),
        P(("groups", "box", "sub")),
        P(None, ("groups", "box"), "sub", None, None),
        P("groups"),
        P("groups"),
        P(("groups", "box"), None),
        P(("groups", "box"), None),
        P(("groups", "box"), None),
        P(("groups", "box"), None),
        P(),
        P(),
        P(),
        P(),
    )
    return jax.shard_map(
        functools.partial(shards, mesh.shape["box"]),
        mesh=mesh,
        in_specs=placed,
        out_specs=P(None, "angle", ("groups", "box"), "sub"),
        check_vma=False,
    )
```

```python
import functools

import jax
import jax.numpy as jnp
from jax import lax
from jax.experimental import pallas as pl
from jax.experimental.pallas import tpu as pltpu
from jax.sharding import PartitionSpec as P

BF16 = jnp.bfloat16
F32 = jnp.float32
MESH = pl.DeviceIdType.MESH


def turned(value):
    half = value.shape[0] // 2
    return jnp.concatenate([-value[half:], value[:half]], axis=0)


def dot(left, right, right_dim):
    return lax.dot_general(
        left, right, (((1,), (right_dim,)), ((), ())), preferred_element_type=F32
    )


def kernel(
    n,
    pairs_hbm,
    count_hbm,
    parent_of_hbm,
    octant_hbm,
    src0_hbm,
    disp0_hbm,
    src1_hbm,
    disp1_hbm,
    currents,
    near_blocks,
    radiation,
    trans0,
    trans1,
    phases,
    interp,
    out,
    pairs,
    count,
    parent_of,
    octant,
    src0,
    disp0,
    src1,
    disp1,
    staged,
    mine,
    pool,
    pool_turned,
    blocks,
    rad,
    table0,
    table1,
    phase,
    cosine,
    sine,
    interp_wide,
    pattern,
    operators,
    lifted,
    down,
    parent,
    forward,
    backward,
    near_sum,
    mirror_out,
    mirror_in,
    half_out,
    half_in,
    local_sem,
    pattern_send,
    pattern_recv,
    operator_send,
    operator_recv,
    next_send,
    next_recv,
    mirror_send,
    mirror_recv,
    half_send,
    half_recv,
):
    me = lax.axis_index("box")
    sub = lax.axis_index("sub")
    slots = currents.shape[1]
    half_rows = currents.shape[2]
    rows = 2 * half_rows
    boxes = pattern.shape[0]
    parents = parent.shape[0]
    parents_here = src1.shape[0]
    slot_count = pairs.shape[1]
    own_start = me * slots

    barrier = pltpu.get_barrier_semaphore()
    for step in range(1, n):
        pl.semaphore_signal(
            barrier, inc=1, device_id={"box": lax.rem(me + step, n)}, device_id_type=MESH
        )
    pl.semaphore_signal(barrier, inc=1, device_id={"sub": 1 - sub}, device_id_type=MESH)

    next_pool = pool.at[pl.ds(slots, slots)]
    sources = (
        currents,
        radiation,
        disp1_hbm,
        src1_hbm,
        trans1,
        phases,
        octant_hbm,
        parent_of_hbm,
        src0_hbm,
        disp0_hbm,
        pairs_hbm,
        count_hbm,
        interp,
        trans0,
        near_blocks,
    )
    targets = (
        staged,
        rad,
        disp1,
        src1,
        table1,
        phase,
        octant,
        parent_of,
        src0,
        disp0,
        pairs,
        count,
        interp_wide,
        table0,
        blocks,
    )
    local = [
        pltpu.make_async_copy(a, b, local_sem.at[i])
        for i, (a, b) in enumerate(zip(sources, targets))
    ]
    for copy in local[:-1]:
        copy.start()
    get_currents, get_rad, *get_parent_lists = local[:5]
    get_phase, *get_lists = local[5:12]
    get_interp, get_table0, get_blocks = local[12:]

    get_currents.wait()
    for b in range(slots):
        wide = jnp.concatenate([staged[0, b].astype(F32), staged[1, b].astype(F32)], axis=0)
        mine[b] = wide.astype(BF16)
        pool[b] = wide.astype(BF16)
        pool_turned[b] = turned(wide).astype(BF16)
    get_rad.wait()
    get_blocks.start()
    own_box = pl.ds(own_start, slots)
    for b in range(slots):
        pattern[own_start + b] = (
            dot(mine[b], rad[0, b, 0], 1) + dot(pool_turned[b], rad[1, b, 0], 1)
        ).astype(BF16)

    pl.semaphore_wait(barrier, n)

    pattern_copies = []
    for step in range(1, n):
        copy = pltpu.make_async_remote_copy(
            src_ref=pattern.at[own_box],
            dst_ref=pattern.at[own_box],
            send_sem=pattern_send.at[step - 1],
            recv_sem=pattern_recv.at[step - 1],
            device_id={"box": lax.rem(me + step, n)},
            device_id_type=MESH,
        )
        copy.start()
        pattern_copies.append(copy)

    next_copy = pltpu.make_async_remote_copy(
        src_ref=mine,
        dst_ref=next_pool,
        send_sem=next_send,
        recv_sem=next_recv,
        device_id={"box": lax.rem(me + n - 1, n)},
        device_id_type=MESH,
    )

    @pl.when(me > 0)
    def _():
        next_copy.start()

    @pl.when(me == n - 1)
    def _():
        pool[pl.ds(slots, slots)] = jnp.zeros((slots,) + pool.shape[1:], BF16)

    for copy in get_parent_lists:
        copy.wait()
    position = lax.broadcasted_iota(jnp.int32, (parents, table1.shape[2]), 0)
    own_operator = pl.ds(me * parents_here, parents_here)
    for r in range(parents_here):
        real = jnp.zeros(position.shape, F32)
        imag = jnp.zeros(position.shape, F32)
        for k in range(src1.shape[1]):
            row = table1[disp1[r, k]].astype(F32)
            hit = position == src1[r, k]
            real = real + jnp.where(hit, row[0:1], 0.0)
            imag = imag + jnp.where(hit, row[1:2], 0.0)
        operators[me * parents_here + r] = jnp.concatenate([real, imag], axis=0).astype(BF16)
    operator_copies = []
    for step in range(1, n):
        copy = pltpu.make_async_remote_copy(
            src_ref=operators.at[own_operator],
            dst_ref=operators.at[own_operator],
            send_sem=operator_send.at[step - 1],
            recv_sem=operator_recv.at[step - 1],
            device_id={"box": lax.rem(me + step, n)},
            device_id_type=MESH,
        )
        copy.start()
        operator_copies.append(copy)

    for copy in get_lists:
        copy.wait()
    get_blocks.wait()

    def backward_step(p, carry):
        target = jnp.clip(pairs[0, p] - own_start, 0, slots - 1)
        backward[p] = dot(mine[target], blocks[0, p], 0) + dot(pool_turned[target], blocks[1, p], 0)
        return carry

    lax.fori_loop(0, slot_count, backward_step, 0, unroll=True)

    def mirror_weight(p, b):
        source = pairs[1, p]
        hit = (source - own_start == b) & (source != pairs[0, p]) & (p < count[0])
        return jnp.where(hit, 1.0, 0.0).astype(F32)

    def target_weight(p, b):
        hit = (pairs[0, p] - own_start == b) & (p < count[0])
        return jnp.where(hit, 1.0, 0.0).astype(F32)

    zero = jnp.zeros(pool.shape[1:], F32)

    def mirror_box(b, carry):
        def step(p, total):
            return total + mirror_weight(p, slots + b) * backward[p]

        mirror_out[b] = lax.fori_loop(0, slot_count, step, zero, unroll=True).astype(BF16)
        return carry

    lax.fori_loop(0, slots, mirror_box, 0, unroll=True)
    mirror_copy = pltpu.make_async_remote_copy(
        src_ref=mirror_out,
        dst_ref=mirror_in,
        send_sem=mirror_send,
        recv_sem=mirror_recv,
        device_id={"box": lax.rem(me + 1, n)},
        device_id_type=MESH,
    )

    @pl.when(me < n - 1)
    def _():
        mirror_copy.start()

    @pl.when(me == 0)
    def _():
        mirror_in[...] = jnp.zeros(mirror_in.shape, BF16)

    get_phase.wait()
    cosine[...] = jnp.cos(phase[...])
    sine[...] = jnp.sin(phase[...])
    get_interp.wait()
    narrow = interp_wide[...].astype(BF16)
    parent[...] = jnp.zeros(parent.shape, F32)
    merged = slots * rows

    def lift_part(part):
        start = part * slots
        part_rows = pattern[pl.ds(start, slots)].reshape(merged, pattern.shape[2])
        up = dot(part_rows, narrow, 1)
        for i in range(slots):
            cos_row = cosine[pl.ds(octant[start + i], 1), :]
            sin_row = sine[pl.ds(octant[start + i], 1), :]
            real = up[i * rows : i * rows + half_rows]
            imag = up[i * rows + half_rows : (i + 1) * rows]
            lifted[i] = jnp.concatenate(
                [real * cos_row - imag * sin_row, real * sin_row + imag * cos_row], axis=0
            )

        def sum_parent(r, carry):
            total = parent[r]
            for i in range(slots):
                weight = jnp.where(parent_of[start + i] == r, 1.0, 0.0).astype(F32)
                total = total + weight * lifted[i]
            parent[r] = total
            return carry

        lax.fori_loop(0, parents, sum_parent, 0, unroll=parents <= 8)

    lift_part(me)

    @pl.when(me < n - 1)
    def _():
        next_copy.wait_recv()

    for b in range(slots, 2 * slots):
        pool_turned[b] = turned(pool[b].astype(F32)).astype(BF16)

    def forward_step(p, carry):
        source = jnp.clip(pairs[1, p] - own_start, 0, 2 * slots - 1)
        forward[p] = dot(pool[source], blocks[0, p], 1) + dot(pool_turned[source], blocks[1, p], 1)
        return carry

    lax.fori_loop(0, slot_count, forward_step, 0, unroll=True)

    def near_box(b, carry):
        def step(p, total):
            total = total + target_weight(p, b) * forward[p]
            return total + mirror_weight(p, b) * backward[p]

        near_sum[b] = lax.fori_loop(0, slot_count, step, zero, unroll=True)
        return carry

    lax.fori_loop(0, slots, near_box, 0, unroll=True)

    for step in sorted(range(1, n), key=lambda k: min(k, n - k)):
        pattern_copies[step - 1].wait_recv()
        lift_part(lax.rem(me + n - step, n))

    for copy in operator_copies:
        copy.wait_recv()
    get_table0.wait()

    def round_parent(r, carry):
        parent[r] = parent[r].astype(BF16).astype(F32)
        return carry

    lax.fori_loop(0, parents, round_parent, 0, unroll=parents <= 8)

    for b in range(slots):
        owner = parent_of[own_start + b]
        pf_real = jnp.zeros((half_rows, parent.shape[2]), F32)
        pf_imag = jnp.zeros((half_rows, parent.shape[2]), F32)
        operator = operators[owner].astype(F32)
        for s in range(parents):
            value = parent[s]
            real, imag = value[:half_rows], value[half_rows:]
            fr = operator[s : s + 1]
            fi = operator[parents + s : parents + s + 1]
            pf_real = pf_real + (real * fr - imag * fi)
            pf_imag = pf_imag + (real * fi + imag * fr)
        pf_real = pf_real.astype(BF16).astype(F32)
        pf_imag = pf_imag.astype(BF16).astype(F32)
        spot = octant[own_start + b]
        cos_row = cosine[pl.ds(spot, 1), :]
        sin_row = sine[pl.ds(spot, 1), :]
        down[b] = jnp.concatenate(
            [pf_real * cos_row + pf_imag * sin_row, pf_imag * cos_row - pf_real * sin_row], axis=0
        ).astype(BF16)
    descended = dot(down[...].reshape(merged, down.shape[2]), narrow, 0)

    quarter = jnp.zeros((half_rows, pattern.shape[2]), F32)
    for b in range(slots):

        def translate(k, total):
            value = pattern[src0[b, k]].astype(F32)
            factor = table0[disp0[b, k]].astype(F32)
            real, imag = value[:half_rows], value[half_rows:]
            fr, fi = factor[0:1], factor[1:2]
            return (total[0] + (real * fr - imag * fi), total[1] + (real * fi + imag * fr))

        far_real, far_imag = lax.fori_loop(
            0, src0.shape[1], translate, (quarter, quarter), unroll=True
        )
        field = jnp.concatenate([far_real, far_imag], axis=0) + descended[b * rows : (b + 1) * rows]
        field = field.astype(BF16)
        wide = turned(field.astype(F32)).astype(BF16)
        near_sum[b] += dot(field, rad[0, b, 0], 0) + dot(wide, rad[1, b, 0], 0)

    @pl.when(me > 0)
    def _():
        mirror_copy.wait_recv()

    cut = out.shape[3]
    kept = []
    for b in range(slots):
        total = near_sum[b] + mirror_in[b].astype(F32)
        low, high = total[:, :cut], total[:, cut:]
        kept.append(jnp.where(sub == 0, low, high))
        half_out[b] = jnp.where(sub == 0, high, low).astype(BF16)
    half_copy = pltpu.make_async_remote_copy(
        src_ref=half_out,
        dst_ref=half_in,
        send_sem=half_send,
        recv_sem=half_recv,
        device_id={"sub": 1 - sub},
        device_id_type=MESH,
    )
    half_copy.start()
    for copy in pattern_copies + operator_copies:
        copy.wait_send()

    @pl.when(me > 0)
    def _():
        next_copy.wait_send()

    @pl.when(me < n - 1)
    def _():
        mirror_copy.wait_send()

    half_copy.wait()
    for b in range(slots):
        total = kept[b] + half_in[b].astype(F32)
        out[0, b] = total[:half_rows].astype(BF16)
        out[1, b] = total[half_rows:].astype(BF16)


def shards(
    n,
    currents,
    near_blocks,
    near_pairs,
    near_count,
    radiation,
    parent_of,
    octant,
    far0_src,
    far0_disp,
    far1_src,
    far1_disp,
    trans0,
    trans1,
    phases,
    interp,
):
    _, angles, slots, unknowns = currents.shape
    rows = 2 * angles
    boxes = parent_of.shape[0]
    parents_here = far1_src.shape[0]
    parents = n * parents_here
    fine, coarse = interp.shape[1], interp.shape[0]
    slot_count = near_pairs.shape[0]
    cut = unknowns // lax.axis_size("sub")
    per_box = jnp.transpose(currents, (0, 2, 1, 3))
    away = pl.BlockSpec(memory_space=pltpu.HBM)
    lists = (near_pairs.T, near_count, parent_of, octant, far0_src, far0_disp, far1_src, far1_disp)
    dma = pltpu.SemaphoreType.DMA
    result = pl.pallas_call(
        functools.partial(kernel, n),
        out_shape=jax.ShapeDtypeStruct((2, slots, angles, cut), BF16),
        in_specs=[away] * 15,
        out_specs=pl.BlockSpec(memory_space=pltpu.VMEM),
        scratch_shapes=[pltpu.SMEM(entry.shape, jnp.int32) for entry in lists]
        + [
            pltpu.VMEM(per_box.shape, BF16),
            pltpu.VMEM((slots, rows, unknowns), BF16),
            pltpu.VMEM((2 * slots, rows, unknowns), BF16),
            pltpu.VMEM((2 * slots, rows, unknowns), BF16),
            pltpu.VMEM(near_blocks.shape, BF16),
            pltpu.VMEM(radiation.shape, BF16),
            pltpu.VMEM(trans0.shape, BF16),
            pltpu.VMEM(trans1.shape, BF16),
            pltpu.VMEM(phases.shape, F32),
            pltpu.VMEM(phases.shape, F32),
            pltpu.VMEM(phases.shape, F32),
            pltpu.VMEM(interp.shape, F32),
            pltpu.VMEM((boxes, rows, fine), BF16),
            pltpu.VMEM((parents, 2 * parents, coarse), BF16),
            pltpu.VMEM((slots, rows, coarse), F32),
            pltpu.VMEM((slots, rows, coarse), BF16),
            pltpu.VMEM((parents, rows, coarse), F32),
            pltpu.VMEM((slot_count, rows, unknowns), F32),
            pltpu.VMEM((slot_count, rows, unknowns), F32),
            pltpu.VMEM((slots, rows, unknowns), F32),
            pltpu.VMEM((slots, rows, unknowns), BF16),
            pltpu.VMEM((slots, rows, unknowns), BF16),
            pltpu.VMEM((slots, rows, cut), BF16),
            pltpu.VMEM((slots, rows, cut), BF16),
            dma((15,)),
            dma((n - 1,)),
            dma((n - 1,)),
            dma((n - 1,)),
            dma((n - 1,)),
            dma,
            dma,
            dma,
            dma,
            dma,
            dma,
        ],
        compiler_params=pltpu.CompilerParams(
            collective_id=0, has_side_effects=True, vmem_limit_bytes=60 * 1024 * 1024
        ),
    )(
        *lists,
        per_box,
        near_blocks,
        radiation,
        trans0,
        trans1,
        phases,
        interp,
    )
    return jnp.transpose(result, (0, 2, 1, 3))


def solution(mesh):
    placed = (
        P(None, "angle", ("groups", "box"), None),
        P(None, ("groups", "box", "sub"), None, None),
        P(("groups", "box", "sub"), None),
        P(("groups", "box", "sub")),
        P(None, ("groups", "box"), "sub", None, None),
        P("groups"),
        P("groups"),
        P(("groups", "box"), None),
        P(("groups", "box"), None),
        P(("groups", "box"), None),
        P(("groups", "box"), None),
        P(),
        P(),
        P(),
        P(),
    )
    return jax.shard_map(
        functools.partial(shards, mesh.shape["box"]),
        mesh=mesh,
        in_specs=placed,
        out_specs=P(None, "angle", ("groups", "box"), "sub"),
        check_vma=False,
    )
```
